32 devices in a mesh: dp: 2 (over core), expert: 16 (over z, y, x).
Axes of the slice: x: 2, y: 2, z: 4, core: 2. Of those that a mesh axis runs over, the one named last changes fastest.
Arguments:
- states: bfloat16 [3, 4096, 1024], P(None, ('dp', 'expert')), may hold values from -6 to 6
- language: int32 [3, 4096, 1], P(None, ('dp', 'expert')), may hold values from 0 to 15; in each aligned block of 128 rows (0 to 127, 128 to 255, ..., all dimensions but the last counted through in order) at most 16 rows name the same one
- placement: int32 [3, 16], replicated, may hold values from 0 to 15, each once within a row
- swap_flags: int32 [16], replicated, may hold values from 0 to 1, as said below
- up_weight: bfloat16 [16, 1024, 4096], P('expert', None, 'dp'), may hold values from -0.1875 to 0.1875
- down_weight: bfloat16 [16, 4096, 1024], P('expert', 'dp'), may hold values from -0.09375 to 0.09375
Outputs:
- updated: bfloat16 [3, 4096, 1024], P(None, ('dp', 'expert'))
The draws below stay inside these ranges and needn't reach their ends.
Inputs may be any that keep to these rules, and one draw needn't show every extreme that they name: In the 128 rows of one device at one step (aligned blocks along the rows), no language id occurs more than 16 times, and some id occurs exactly 16 times. `placement`: each step's row is a permutation of the devices of the expert axis. swap_flags[j] equals swap_flags[j + 8] for j under 16/2.
All inputs are finite; a program needn't handle non-finite values.
Results may differ from the reference program's by a relative error of at most 0.0047.
Values may be sent and summed in bfloat16 or wider, within the bound.
A program may use at most 128 MiB of HBM per device.

```python
import math
import jax
import jax.numpy as jnp
import numpy as np
from jax import lax

D = 1024
HID = 4096
ROWS_DEV = 128
STEPS = 3
EXPERTS = 16
LANGS = 16
CAP = 16
TOKENS = 4096
N_DP = 2
N_EXPERT = 16


def draw_swap_flags(key, part):
    first_half = jax.random.randint(key, (EXPERTS // 2,), 0, 2, dtype=jnp.int32)
    return jnp.concatenate([first_half, first_half])


def steps_of(key, extent, split, low, largest):
    factor_of, own = 1.0, jax.random.fold_in(key, 6)
    for dim, shards_of in split:
        heights = jnp.exp(jax.random.uniform(jax.random.fold_in(own, dim), (shards_of,), jnp.float32, low / len(split), largest / len(split)))
        factor_of = factor_of * jnp.repeat(heights, extent[dim] // shards_of).reshape([-1 if axis == dim else 1 for axis in range(len(extent))])
    return factor_of


def assign_block(rng, own, number, rows, amount, top, reach, skew):
    order = jax.random.permutation(rng, amount)
    crowded, ordinary = portions_of(amount, rows * top, reach, skew, True), portions_of(amount, rows * top, reach, skew, False)
    places = jnp.arange(amount)

    def named(sizes, rotation):
        used = int((sizes > 0).sum())
        fixed = max(1, used // 4)
        moved = fixed + (places - fixed + rotation * (used - fixed)) % max(1, amount - fixed)
        return jnp.zeros((amount,), jnp.int32).at[order[jnp.where(places < fixed, places, moved)]].set(jnp.asarray(sizes, jnp.int32))

    sizes = jnp.where(number % 4 == 0, named(crowded, number // 4), named(ordinary, number - number // 4 - 1))
    mixed = jax.random.permutation(jax.random.fold_in(own, 3), amount)
    giver, sink = mixed[0:amount // 2 * 2:2], mixed[1:amount // 2 * 2:2]
    slack = jnp.minimum(sizes[giver] - 1, reach - sizes[sink]) // 2
    slack = jnp.where((giver == order[0]) | (sink == order[0]) | (sizes[sink] == 0), 0, jnp.maximum(slack, 0))
    moved = jax.random.randint(jax.random.fold_in(own, 4), (amount // 2,), 0, 1 << 20) % (slack + 1)
    sizes = sizes.at[giver].add(-moved).at[sink].add(moved)
    items = jnp.searchsorted(jnp.cumsum(sizes), jnp.arange(rows * top), side="right").astype(jnp.int32)
    table = items.reshape(top, rows).T
    table = table[jax.random.permutation(jax.random.fold_in(own, 1), rows)]
    rotation = jax.random.randint(jax.random.fold_in(own, 2), (rows, 1), 0, top)
    return jnp.take_along_axis(table, (jnp.arange(top)[None, :] + rotation) % top, axis=1)


def portions_of(number_of, total, most, slope, full):
    portions = [(1 << 20) // math.isqrt(rank ** slope) + 1 for rank in range(1, number_of + 1)]
    largest = most if full else min(most, max(-(-total // number_of), total * portions[0] // sum(portions)))
    least = 1 if total - largest >= number_of - 1 else 0
    holding, spare = [largest] + [least] * (number_of - 1), total - largest - least * (number_of - 1)
    while spare > 0:
        movable = [i for i in range(1, number_of) if holding[i] < largest] or [i for i in range(1, number_of) if holding[i] < most]
        mass, budget = sum([portions[i] for i in movable]), spare
        for i in movable:
            addition = min(most - holding[i], max(1, budget * portions[i] // mass), spare)
            holding[i] = holding[i] + addition
            spare = spare - addition
    return np.array(holding)


def scatter_about(own_key, dims, spread, most, cuts=(), kind=jnp.bfloat16):
    factor_of = steps_of(own_key, dims, cuts, -0.22, 0.18) if cuts else 1.0
    array = jax.random.normal(own_key, dims, jnp.float32) * spread * factor_of
    return jnp.minimum(jnp.maximum(array, -most), most).astype(kind)


def setup_inputs(seed: int = 0) -> dict:
    streams_of = jax.random.split(jax.random.key(seed), 7)
    states = scatter_about(streams_of[0], (STEPS, TOKENS, D), 1.0, 6.0, ((1, 32),))
    language_keys = jax.random.split(jax.random.fold_in(streams_of[1], 1), STEPS * TOKENS // ROWS_DEV)
    language_turns = jax.random.permutation(jax.random.fold_in(streams_of[1], 3), STEPS * TOKENS // ROWS_DEV)
    language = jax.vmap(lambda own, number: assign_block(jax.random.fold_in(streams_of[1], 2), own, number, ROWS_DEV, LANGS, 1, CAP, 2))(language_keys, language_turns).reshape((STEPS, TOKENS, 1))
    placement = jax.vmap(lambda own: jax.random.permutation(own, EXPERTS))(jax.random.split(streams_of[2], STEPS)).reshape((STEPS, LANGS)).astype(jnp.int32)
    swap_flags = draw_swap_flags(jax.random.fold_in(streams_of[6], 71), 0)
    up_weight = scatter_about(streams_of[4], (EXPERTS, D, HID), D ** -0.5, 0.1875, ((0, 16), (2, 2)))
    down_weight = scatter_about(streams_of[5], (EXPERTS, HID, D), HID ** -0.5, 0.09375, ((0, 16), (1, 2)))
    return dict(states=states, language=language, placement=placement, swap_flags=swap_flags, up_weight=up_weight, down_weight=down_weight)


def feed_forward(row_block, up_matrix, down_matrix):
    hidden = jnp.maximum(jnp.dot(row_block, up_matrix, preferred_element_type=jnp.float32), 0.0).astype(jnp.bfloat16)
    return jnp.dot(hidden, down_matrix, preferred_element_type=jnp.float32).astype(jnp.bfloat16)


def serve_rows(row_states, served, up_weight, down_weight):
    labels = jnp.arange(EXPERTS, dtype=jnp.int32)
    counts = jnp.sum((served[:, None] == labels[None, :]).astype(jnp.int32), axis=0).astype(jnp.int32)
    starts = (jnp.cumsum(counts) - counts).astype(jnp.int32)
    row_order = jnp.argsort(served, stable=True).astype(jnp.int32)
    sorted_rows = row_states[row_order]
    offsets = jnp.arange(CAP * N_DP * N_EXPERT, dtype=jnp.int32)

    def one_expert(running, expert):
        positions = jnp.minimum(starts[expert] + offsets, TOKENS - 1).astype(jnp.int32)
        is_filled = offsets < counts[expert]
        row_block = sorted_rows[positions]
        up_matrix = lax.dynamic_index_in_dim(up_weight, expert, 0, keepdims=False)
        down_matrix = lax.dynamic_index_in_dim(down_weight, expert, 0, keepdims=False)
        expert_out = feed_forward(row_block, up_matrix, down_matrix).astype(jnp.float32)
        running = running.at[positions].add(jnp.where(is_filled[:, None], expert_out, jnp.zeros_like(expert_out)))
        return running, None

    zero_rows = jnp.zeros((TOKENS, D), jnp.float32)
    gathered_sum, unused = lax.scan(one_expert, zero_rows, labels)
    return jnp.zeros((TOKENS, D), jnp.float32).at[row_order].set(gathered_sum)


def reference(states, language, placement, swap_flags, up_weight, down_weight):
    labels = jnp.arange(EXPERTS, dtype=jnp.int32)
    resident = jnp.where(swap_flags == 1, (labels + EXPERTS // 2) % EXPERTS, labels).astype(jnp.int32)
    outputs = []
    for step_index in range(STEPS):
        served = placement[step_index][language[step_index, :, 0]].astype(jnp.int32)
        if step_index >= 1:
            served = resident[served].astype(jnp.int32)
        update = serve_rows(states[step_index], served, up_weight, down_weight)
        outputs.append((states[step_index].astype(jnp.float32) + update).astype(jnp.bfloat16))
    return jnp.stack(outputs)
```

```python
import functools

import jax
import jax.numpy as jnp
from jax import lax
from jax.experimental import pallas as pl
from jax.experimental.pallas import tpu as pltpu
from jax.sharding import PartitionSpec as P

MESH = pl.DeviceIdType.MESH
PIECE = 512


def slots_of(language, placement, swap_flags, experts, capacity):
    labels = jnp.arange(experts, dtype=jnp.int32)
    resident = jnp.where(swap_flags == 1, (labels + experts // 2) % experts, labels)
    moved = jnp.sum(jnp.where(placement[:, :, None] == labels, resident, 0), axis=2)
    steps = jnp.arange(placement.shape[0], dtype=jnp.int32)[:, None]
    device_of = jnp.where(steps == 0, placement, moved)
    ids = language[:, :, 0]
    target = jnp.sum(jnp.where(ids[:, :, None] == labels, device_of[:, None, :], 0), axis=2)
    rows = jnp.arange(ids.shape[1], dtype=jnp.int32)
    earlier = (ids[:, :, None] == ids[:, None, :]) & (rows[None, :] < rows[:, None])
    return target * capacity + jnp.sum(earlier.astype(jnp.int32), axis=2)


def layer_kernel(
    slot_row, slot_col, states, up, down, out,
    up_all, down_all, outgoing, arrived, results, returned, total,
    own_sem, half_send, half_recv, go_send, go_recv, back_send, back_recv,
):
    steps, experts, capacity, width = outgoing.shape
    pieces = up_all.shape[0] // 2
    rows = states.shape[1]
    slots = experts * capacity
    core, me = lax.axis_index("dp"), lax.axis_index("expert")
    other = 1 - core

    def peer(k):
        return lax.rem(me + k, experts)

    def over_peers(body):
        def step_of(k, carry):
            body(peer(k))
            return carry
        lax.fori_loop(1, experts, step_of, 0)

    def own_copies(piece):
        columns = pl.ds(piece * PIECE, PIECE)
        return (
            pltpu.make_async_copy(up.at[:, columns], up_all.at[piece], own_sem.at[0, piece]),
            pltpu.make_async_copy(down.at[columns, :], down_all.at[piece], own_sem.at[1, piece]),
        )

    def half_copies(piece):
        columns = pl.ds(piece * PIECE, PIECE)
        ends = dict(device_id=(other, me), device_id_type=MESH)
        return (
            pltpu.make_async_remote_copy(
                up.at[:, columns], up_all.at[pieces + piece], half_send.at[0, piece], half_recv.at[0, piece], **ends),
            pltpu.make_async_remote_copy(
                down.at[columns, :], down_all.at[pieces + piece], half_send.at[1, piece], half_recv.at[1, piece], **ends),
        )

    def go_copy(step, device):
        return pltpu.make_async_remote_copy(
            outgoing.at[step, device], arrived.at[step, me], go_send.at[step, device], go_recv.at[step, me],
            device_id=(core, device), device_id_type=MESH)

    def go_arrival(step, device):
        return pltpu.make_async_remote_copy(
            outgoing.at[step, device], arrived.at[step, device], go_send.at[step, device], go_recv.at[step, device],
            device_id=(core, device), device_id_type=MESH)

    def back_copy(step, device):
        return pltpu.make_async_remote_copy(
            results.at[step, device], returned.at[step, me], back_send.at[step, device], back_recv.at[step, me],
            device_id=(core, device), device_id_type=MESH)

    def back_arrival(step, device):
        return pltpu.make_async_remote_copy(
            results.at[step, device], returned.at[step, device], back_send.at[step, device], back_recv.at[step, device],
            device_id=(core, device), device_id_type=MESH)

    for piece in range(pieces):
        for copy in own_copies(piece):
            copy.start()

    barrier = pltpu.get_barrier_semaphore()
    over_peers(lambda device: pl.semaphore_signal(
        barrier, inc=1, device_id=(core, device), device_id_type=MESH))
    pl.semaphore_signal(barrier, inc=1, device_id=(other, me), device_id_type=MESH)

    def fill(step):
        place = lax.broadcasted_iota(jnp.int32, (slots, rows), 0)
        pick = (place == slot_row[step]).astype(jnp.bfloat16)
        rows_out = jnp.dot(pick, states[step], preferred_element_type=jnp.float32)
        outgoing[step] = rows_out.astype(jnp.bfloat16).reshape(experts, capacity, width)

    fill(0)
    pl.semaphore_wait(barrier, experts)
    for step in range(steps):
        if step:
            fill(step)
        over_peers(lambda device: go_copy(step, device).start())
        if step == 0:
            for piece in range(pieces):
                for copy in half_copies(piece):
                    copy.start()
        arrived[step, me] = outgoing[step, me]

    def add_piece(step, piece, first):
        x = arrived[step].reshape(slots, width)
        hidden = jnp.dot(x, up_all[piece], preferred_element_type=jnp.float32)
        hidden = jnp.maximum(hidden, 0.0).astype(jnp.bfloat16)
        term = jnp.dot(hidden, down_all[piece], preferred_element_type=jnp.float32)
        if first:
            total[...] = term
        else:
            total[...] += term

    def combine(step):
        over_peers(lambda device: back_arrival(step, device).wait_recv())
        place = lax.broadcasted_iota(jnp.int32, (rows, slots), 1)
        pick = (place == slot_col[step]).astype(jnp.bfloat16)
        update = jnp.dot(
            pick, returned[step].reshape(slots, width), preferred_element_type=jnp.float32)
        out[step] = (states[step].astype(jnp.float32) + update).astype(jnp.bfloat16)

    for step in range(steps):
        over_peers(lambda device: go_arrival(step, device).wait_recv())
        for piece in range(2 * pieces):
            if step == 0:
                if piece < pieces:
                    for copy in own_copies(piece):
                        copy.wait()
                else:
                    for copy in half_copies(piece - pieces):
                        copy.wait_recv()
            add_piece(step, piece, piece == 0)
        results[step] = total[...].astype(jnp.bfloat16).reshape(experts, capacity, width)
        over_peers(lambda device: back_copy(step, device).start())
        returned[step, me] = results[step, me]
    for step in range(steps):
        combine(step)

    for piece in range(pieces):
        for copy in half_copies(piece):
            copy.wait_send()
    for step in range(steps):
        over_peers(lambda device: go_copy(step, device).wait_send())
        over_peers(lambda device: back_copy(step, device).wait_send())


def kernel_layer(states, slot_index, up_local, down_local, experts, capacity):
    steps, rows, width = states.shape
    pieces = up_local.shape[1] // PIECE
    blocks = pltpu.VMEM((steps, experts, capacity, width), jnp.bfloat16)
    sems = pltpu.SemaphoreType.DMA
    vmem = pl.BlockSpec(memory_space=pltpu.VMEM)
    anywhere = pl.BlockSpec(memory_space=pl.ANY)
    return pl.pallas_call(
        layer_kernel,
        out_shape=jax.ShapeDtypeStruct((steps, rows, width), jnp.bfloat16),
        in_specs=[vmem, vmem, vmem, anywhere, anywhere],
        out_specs=vmem,
        scratch_shapes=[
            pltpu.VMEM((2 * pieces, width, PIECE), jnp.bfloat16),
            pltpu.VMEM((2 * pieces, PIECE, width), jnp.bfloat16),
            blocks, blocks, blocks, blocks,
            pltpu.VMEM((experts * capacity, width), jnp.float32),
            sems((2, pieces)), sems((2, pieces)), sems((2, pieces)),
            sems((steps, experts)), sems((steps, experts)),
            sems((steps, experts)), sems((steps, experts)),
        ],
        compiler_params=pltpu.CompilerParams(
            collective_id=0, has_side_effects=True, vmem_limit_bytes=56 * 2**20),
        cost_estimate=pl.CostEstimate(
            flops=8 * steps * experts * capacity * width * up_local.shape[1],
            bytes_accessed=4 * up_local.size * 2, transcendentals=0),
    )(slot_index[:, None, :], slot_index[:, :, None], states, up_local, down_local)


def plain_layer(states, slot_index, up_local, down_local, experts, capacity):
    width = states.shape[2]
    slot_labels = jnp.arange(experts * capacity, dtype=jnp.int32)
    outputs = []
    for step in range(states.shape[0]):
        select = (slot_index[step][:, None] == slot_labels[None, :]).astype(jnp.bfloat16)
        outgoing = jnp.einsum("rs,rd->sd", select, states[step], preferred_element_type=jnp.float32)
        arrived = lax.all_to_all(
            outgoing.astype(jnp.bfloat16).reshape(experts, capacity, width),
            "expert", split_axis=0, concat_axis=0, tiled=True)
        both = lax.all_gather(
            arrived.reshape(experts * capacity, width), "dp", axis=0, tiled=True)
        hidden = jnp.maximum(jnp.dot(both, up_local, preferred_element_type=jnp.float32), 0.0)
        terms = jnp.dot(hidden.astype(jnp.bfloat16), down_local, preferred_element_type=jnp.float32)
        served = lax.psum_scatter(terms, "dp", scatter_dimension=0, tiled=True).astype(jnp.bfloat16)
        returned = lax.all_to_all(
            served.reshape(experts, capacity, width), "expert", split_axis=0, concat_axis=0, tiled=True)
        update = jnp.dot(
            select, returned.reshape(experts * capacity, width), preferred_element_type=jnp.float32)
        outputs.append((states[step].astype(jnp.float32) + update).astype(jnp.bfloat16))
    return jnp.stack(outputs)


def shards(states, language, placement, swap_flags, up_weight, down_weight):
    experts = lax.axis_size("expert")
    capacity = max(2, 2 * states.shape[1] // experts)
    slot_index = slots_of(language, placement, swap_flags, experts, capacity)
    layer = kernel_layer if capacity % 16 == 0 else plain_layer
    return layer(states, slot_index, up_weight[0], down_weight[0], experts, capacity)


def solution(mesh):
    rows_by = P(None, ("dp", "expert"), None)
    return jax.shard_map(
        shards,
        mesh=mesh,
        in_specs=(rows_by, rows_by, P(), P(), P("expert", None, "dp"), P("expert", "dp", None)),
        out_specs=rows_by,
        check_vma=False,
    )
```

```python
import jax
import jax.numpy as jnp
from jax import lax
from jax.experimental import pallas as pl
from jax.experimental.pallas import tpu as pltpu
from jax.sharding import PartitionSpec as P

MESH = pl.DeviceIdType.MESH
PIECE = 512


def slots_of(language, placement, swap_flags, experts, capacity):
    labels = jnp.arange(experts, dtype=jnp.int32)
    resident = jnp.where(swap_flags == 1, (labels + experts // 2) % experts, labels)
    moved = jnp.sum(jnp.where(placement[:, :, None] == labels, resident, 0), axis=2)
    steps = jnp.arange(placement.shape[0], dtype=jnp.int32)[:, None]
    device_of = jnp.where(steps == 0, placement, moved)
    ids = language[:, :, 0]
    target = jnp.sum(jnp.where(ids[:, :, None] == labels, device_of[:, None, :], 0), axis=2)
    rows = jnp.arange(ids.shape[1], dtype=jnp.int32)
    earlier = (ids[:, :, None] == ids[:, None, :]) & (rows[None, :] < rows[:, None])
    return target * capacity + jnp.sum(earlier.astype(jnp.int32), axis=2)


def layer_kernel(
    language, placement, swap_flags, states, up, down, out,
    up_all, down_all, outgoing, arrived, results, returned, picks, total,
    own_sem, half_send, half_recv, go_send, go_recv, back_send, back_recv,
):
    steps, experts, capacity, width = outgoing.shape
    pieces = up_all.shape[0] // 2
    rows = states.shape[1]
    slots = experts * capacity
    core, me = lax.axis_index("dp"), lax.axis_index("expert")
    other = 1 - core

    def peer(k):
        return lax.rem(me + k, experts)

    def over_peers(body):
        def step_of(k, carry):
            body(peer(k))
            return carry
        lax.fori_loop(1, experts, step_of, 0)

    def own_copies(piece):
        columns = pl.ds(piece * PIECE, PIECE)
        return (
            pltpu.make_async_copy(up.at[:, columns], up_all.at[piece], own_sem.at[0, piece]),
            pltpu.make_async_copy(down.at[columns, :], down_all.at[piece], own_sem.at[1, piece]),
        )

    def half_copies(piece):
        columns = pl.ds(piece * PIECE, PIECE)
        ends = dict(device_id=(other, me), device_id_type=MESH)
        return (
            pltpu.make_async_remote_copy(
                up.at[:, columns], up_all.at[pieces + piece], half_send.at[0, piece], half_recv.at[0, piece], **ends),
            pltpu.make_async_remote_copy(
                down.at[columns, :], down_all.at[pieces + piece], half_send.at[1, piece], half_recv.at[1, piece], **ends),
        )

    def go_copy(step, device):
        return pltpu.make_async_remote_copy(
            outgoing.at[step, device], arrived.at[step, me], go_send.at[step, device], go_recv.at[step, me],
            device_id=(core, device), device_id_type=MESH)

    def go_arrival(step, device):
        return pltpu.make_async_remote_copy(
            outgoing.at[step, device], arrived.at[step, device], go_send.at[step, device], go_recv.at[step, device],
            device_id=(core, device), device_id_type=MESH)

    def back_copy(step, device):
        return pltpu.make_async_remote_copy(
            results.at[step, device], returned.at[step, me], back_send.at[step, device], back_recv.at[step, me],
            device_id=(core, device), device_id_type=MESH)

    def back_arrival(step, device):
        return pltpu.make_async_remote_copy(
            results.at[step, device], returned.at[step, device], back_send.at[step, device], back_recv.at[step, device],
            device_id=(core, device), device_id_type=MESH)

    barrier = pltpu.get_barrier_semaphore()
    over_peers(lambda device: pl.semaphore_signal(
        barrier, inc=1, device_id=(core, device), device_id_type=MESH))
    pl.semaphore_signal(barrier, inc=1, device_id=(other, me), device_id_type=MESH)

    def fill(step):
        langs = placement.shape[1]
        label = lax.broadcasted_iota(jnp.int32, (langs, langs), 0)
        along = lax.broadcasted_iota(jnp.int32, (langs, langs), 1)
        served_by = placement[pl.ds(step, 1), :].astype(jnp.float32)
        target = jnp.sum(jnp.where(label == along, served_by, 0.0), axis=1, keepdims=True)
        if step:
            flags = swap_flags[...].astype(jnp.float32)
            flag = jnp.sum(
                jnp.where(along.astype(jnp.float32) == target, flags, 0.0), axis=1, keepdims=True)
            half = experts // 2
            traded = jnp.where(target < half, target + half, target - half)
            target = jnp.where(flag > 0.5, traded, target)
        hot = lax.broadcasted_iota(jnp.int32, (langs, rows), 0) == language[step]
        before = (lax.broadcasted_iota(jnp.int32, (rows, rows), 0)
                  < lax.broadcasted_iota(jnp.int32, (rows, rows), 1))
        earlier = jnp.dot(
            hot.astype(jnp.bfloat16), before.astype(jnp.bfloat16), preferred_element_type=jnp.float32)
        slot = jnp.sum(jnp.where(hot, target * capacity + earlier, 0.0), axis=0, keepdims=True)
        place = lax.broadcasted_iota(jnp.int32, (slots, rows), 0)
        pick = (place == slot.astype(jnp.int32)).astype(jnp.bfloat16)
        picks[step] = pick
        rows_out = jnp.dot(pick, states[step], preferred_element_type=jnp.float32)
        outgoing[step] = rows_out.astype(jnp.bfloat16).reshape(experts, capacity, width)

    fill(0)
    pl.semaphore_wait(barrier, experts)
    for step in range(steps):
        if step:
            fill(step)
        over_peers(lambda device: go_copy(step, device).start())
        if step == 0:
            for piece in range(pieces):
                for copy in own_copies(piece) + half_copies(piece):
                    copy.start()
        arrived[step, me] = outgoing[step, me]

    def add_piece(step, piece, first):
        x = arrived[step].reshape(slots, width)
        hidden = jnp.dot(x, up_all[piece], preferred_element_type=jnp.float32)
        hidden = jnp.maximum(hidden, 0.0).astype(jnp.bfloat16)
        term = jnp.dot(hidden, down_all[piece], preferred_element_type=jnp.float32)
        if first:
            total[...] = term
        else:
            total[...] += term

    def combine(step):
        over_peers(lambda device: back_arrival(step, device).wait_recv())
        update = lax.dot_general(
            picks[step], returned[step].reshape(slots, width), (((0,), (0,)), ((), ())),
            preferred_element_type=jnp.float32)
        out[step] = update.astype(jnp.bfloat16)

    for step in range(steps):
        over_peers(lambda device: go_arrival(step, device).wait_recv())
        for piece in range(2 * pieces):
            if step == 0:
                if piece < pieces:
                    for copy in own_copies(piece):
                        copy.wait()
                else:
                    for copy in half_copies(piece - pieces):
                        copy.wait_recv()
            add_piece(step, piece, piece == 0)
        results[step] = total[...].astype(jnp.bfloat16).reshape(experts, capacity, width)
        over_peers(lambda device: back_copy(step, device).start())
        returned[step, me] = results[step, me]
    for step in range(steps):
        combine(step)

    for piece in range(pieces):
        for copy in half_copies(piece):
            copy.wait_send()
    for step in range(steps):
        over_peers(lambda device: go_copy(step, device).wait_send())
        over_peers(lambda device: back_copy(step, device).wait_send())


def kernel_layer(states, language, placement, swap_flags, up_local, down_local, experts, capacity):
    steps, rows, width = states.shape
    pieces = up_local.shape[1] // PIECE
    blocks = pltpu.VMEM((steps, experts, capacity, width), jnp.bfloat16)
    sems = pltpu.SemaphoreType.DMA
    vmem = pl.BlockSpec(memory_space=pltpu.VMEM)
    anywhere = pl.BlockSpec(memory_space=pl.ANY)
    update = pl.pallas_call(
        layer_kernel,
        out_shape=jax.ShapeDtypeStruct((steps, rows, width), jnp.bfloat16),
        in_specs=[vmem, vmem, vmem, vmem, anywhere, anywhere],
        out_specs=vmem,
        scratch_shapes=[
            pltpu.VMEM((2 * pieces, width, PIECE), jnp.bfloat16),
            pltpu.VMEM((2 * pieces, PIECE, width), jnp.bfloat16),
            blocks, blocks, blocks, blocks,
            pltpu.VMEM((steps, experts * capacity, rows), jnp.bfloat16),
            pltpu.VMEM((experts * capacity, width), jnp.float32),
            sems((2, pieces)), sems((2, pieces)), sems((2, pieces)),
            sems((steps, experts)), sems((steps, experts)),
            sems((steps, experts)), sems((steps, experts)),
        ],
        compiler_params=pltpu.CompilerParams(
            collective_id=0, has_side_effects=True, vmem_limit_bytes=56 * 2**20),
        cost_estimate=pl.CostEstimate(
            flops=8 * steps * experts * capacity * width * up_local.shape[1],
            bytes_accessed=4 * up_local.size * 2, transcendentals=0),
    )(language.reshape(steps, 1, rows), placement, swap_flags[None, :], states, up_local, down_local)
    return (states.astype(jnp.float32) + update.astype(jnp.float32)).astype(jnp.bfloat16)


def plain_layer(states, language, placement, swap_flags, up_local, down_local, experts, capacity):
    slot_index = slots_of(language, placement, swap_flags, experts, capacity)
    width = states.shape[2]
    slot_labels = jnp.arange(experts * capacity, dtype=jnp.int32)
    outputs = []
    for step in range(states.shape[0]):
        select = (slot_index[step][:, None] == slot_labels[None, :]).astype(jnp.bfloat16)
        outgoing = jnp.einsum("rs,rd->sd", select, states[step], preferred_element_type=jnp.float32)
        arrived = lax.all_to_all(
            outgoing.astype(jnp.bfloat16).reshape(experts, capacity, width),
            "expert", split_axis=0, concat_axis=0, tiled=True)
        both = lax.all_gather(
            arrived.reshape(experts * capacity, width), "dp", axis=0, tiled=True)
        hidden = jnp.maximum(jnp.dot(both, up_local, preferred_element_type=jnp.float32), 0.0)
        terms = jnp.dot(hidden.astype(jnp.bfloat16), down_local, preferred_element_type=jnp.float32)
        served = lax.psum_scatter(terms, "dp", scatter_dimension=0, tiled=True).astype(jnp.bfloat16)
        returned = lax.all_to_all(
            served.reshape(experts, capacity, width), "expert", split_axis=0, concat_axis=0, tiled=True)
        update = jnp.dot(
            select, returned.reshape(experts * capacity, width), preferred_element_type=jnp.float32)
        outputs.append((states[step].astype(jnp.float32) + update).astype(jnp.bfloat16))
    return jnp.stack(outputs)


def shards(states, language, placement, swap_flags, up_weight, down_weight):
    experts = lax.axis_size("expert")
    capacity = max(2, 2 * states.shape[1] // experts)
    layer = kernel_layer if capacity % 16 == 0 else plain_layer
    return layer(states, language, placement, swap_flags, up_weight[0], down_weight[0], experts, capacity)


def solution(mesh):
    rows_by = P(None, ("dp", "expert"), None)
    return jax.shard_map(
        shards,
        mesh=mesh,
        in_specs=(rows_by, rows_by, P(), P(), P("expert", None, "dp"), P("expert", "dp", None)),
        out_specs=rows_by,
        check_vma=False,
    )
```

```python
import jax
import jax.numpy as jnp
from jax import lax
from jax.experimental import pallas as pl
from jax.experimental.pallas import tpu as pltpu
from jax.sharding import PartitionSpec as P

MESH = pl.DeviceIdType.MESH
PIECE = 512


def slots_of(language, placement, swap_flags, experts, capacity):
    labels = jnp.arange(experts, dtype=jnp.int32)
    resident = jnp.where(swap_flags == 1, (labels + experts // 2) % experts, labels)
    moved = jnp.sum(jnp.where(placement[:, :, None] == labels, resident, 0), axis=2)
    steps = jnp.arange(placement.shape[0], dtype=jnp.int32)[:, None]
    device_of = jnp.where(steps == 0, placement, moved)
    ids = language[:, :, 0]
    target = jnp.sum(jnp.where(ids[:, :, None] == labels, device_of[:, None, :], 0), axis=2)
    rows = jnp.arange(ids.shape[1], dtype=jnp.int32)
    earlier = (ids[:, :, None] == ids[:, None, :]) & (rows[None, :] < rows[:, None])
    return target * capacity + jnp.sum(earlier.astype(jnp.int32), axis=2)


def layer_kernel(
    language, placement, swap_flags, states, up, down, out,
    up_all, down_all, outgoing, arrived, results, returned, picks, total,
    own_sem, half_send, half_recv, go_send, go_recv, back_send, back_recv,
):
    steps, experts, capacity, width = outgoing.shape
    pieces = up_all.shape[0] // 2
    rows = states.shape[1]
    slots = experts * capacity
    core, me = lax.axis_index("dp"), lax.axis_index("expert")
    other = 1 - core

    def peer(turn):
        if experts & (experts - 1):
            return lax.rem(me + turn + 1, experts)
        offset = (1 - lax.rem(turn, 2)) * (experts // 2) + lax.div(turn + 1, 2)
        device, bit = 0, 1
        while bit < experts:
            device += lax.rem(lax.div(me, bit) + lax.div(offset, bit), 2) * bit
            bit *= 2
        return device

    def over_peers(body):
        def step_of(turn, carry):
            body(peer(turn))
            return carry
        lax.fori_loop(0, experts - 1, step_of, 0)

    def own_copies(piece):
        columns = pl.ds(piece * PIECE, PIECE)
        return (
            pltpu.make_async_copy(up.at[:, columns], up_all.at[piece], own_sem.at[0, piece]),
            pltpu.make_async_copy(down.at[columns, :], down_all.at[piece], own_sem.at[1, piece]),
        )

    def half_copies(piece):
        columns = pl.ds(piece * PIECE, PIECE)
        ends = dict(device_id=(other, me), device_id_type=MESH)
        return (
            pltpu.make_async_remote_copy(
                up.at[:, columns], up_all.at[pieces + piece], half_send.at[0, piece], half_recv.at[0, piece], **ends),
            pltpu.make_async_remote_copy(
                down.at[columns, :], down_all.at[pieces + piece], half_send.at[1, piece], half_recv.at[1, piece], **ends),
        )

    def go_copy(step, device):
        return pltpu.make_async_remote_copy(
            outgoing.at[step, device], arrived.at[step, me], go_send.at[step, device], go_recv.at[step, me],
            device_id=(core, device), device_id_type=MESH)

    def go_arrival(step, device):
        return pltpu.make_async_remote_copy(
            outgoing.at[step, device], arrived.at[step, device], go_send.at[step, device], go_recv.at[step, device],
            device_id=(core, device), device_id_type=MESH)

    def back_copy(step, device):
        return pltpu.make_async_remote_copy(
            results.at[step, device], returned.at[step, me], back_send.at[step, device], back_recv.at[step, me],
            device_id=(core, device), device_id_type=MESH)

    def back_arrival(step, device):
        return pltpu.make_async_remote_copy(
            results.at[step, device], returned.at[step, device], back_send.at[step, device], back_recv.at[step, device],
            device_id=(core, device), device_id_type=MESH)

    barrier = pltpu.get_barrier_semaphore()
    over_peers(lambda device: pl.semaphore_signal(
        barrier, inc=1, device_id=(core, device), device_id_type=MESH))
    pl.semaphore_signal(barrier, inc=1, device_id=(other, me), device_id_type=MESH)

    def fill(step):
        langs = placement.shape[1]
        label = lax.broadcasted_iota(jnp.int32, (langs, langs), 0)
        along = lax.broadcasted_iota(jnp.int32, (langs, langs), 1)
        served_by = placement[pl.ds(step, 1), :].astype(jnp.float32)
        target = jnp.sum(jnp.where(label == along, served_by, 0.0), axis=1, keepdims=True)
        if step:
            flags = swap_flags[...].astype(jnp.float32)
            flag = jnp.sum(
                jnp.where(along.astype(jnp.float32) == target, flags, 0.0), axis=1, keepdims=True)
            half = experts // 2
            traded = jnp.where(target < half, target + half, target - half)
            target = jnp.where(flag > 0.5, traded, target)
        hot = lax.broadcasted_iota(jnp.int32, (langs, rows), 0) == language[step]
        before = (lax.broadcasted_iota(jnp.int32, (rows, rows), 0)
                  < lax.broadcasted_iota(jnp.int32, (rows, rows), 1))
        earlier = jnp.dot(
            hot.astype(jnp.bfloat16), before.astype(jnp.bfloat16), preferred_element_type=jnp.float32)
        slot = jnp.sum(jnp.where(hot, target * capacity + earlier, 0.0), axis=0, keepdims=True)
        place = lax.broadcasted_iota(jnp.int32, (slots, rows), 0)
        pick = (place == slot.astype(jnp.int32)).astype(jnp.bfloat16)
        picks[step] = pick
        rows_out = jnp.dot(pick, states[step], preferred_element_type=jnp.float32)
        outgoing[step] = rows_out.astype(jnp.bfloat16).reshape(experts, capacity, width)

    fill(0)
    pl.semaphore_wait(barrier, experts)
    for step in range(steps):
        if step:
            fill(step)
        over_peers(lambda device: go_copy(step, device).start())
        if step == 0:
            for piece in range(pieces):
                for copy in own_copies(piece) + half_copies(piece):
                    copy.start()
        arrived[step, me] = outgoing[step, me]

    def add_piece(step, piece, first):
        x = arrived[step].reshape(slots, width)
        hidden = jnp.dot(x, up_all[piece], preferred_element_type=jnp.float32)
        hidden = jnp.maximum(hidden, 0.0).astype(jnp.bfloat16)
        term = jnp.dot(hidden, down_all[piece], preferred_element_type=jnp.float32)
        if first:
            total[...] = term
        else:
            total[...] += term

    def combine(step):
        over_peers(lambda device: back_arrival(step, device).wait_recv())
        update = lax.dot_general(
            picks[step], returned[step].reshape(slots, width), (((0,), (0,)), ((), ())),
            preferred_element_type=jnp.float32)
        out[step] = update.astype(jnp.bfloat16)

    for step in range(steps):
        over_peers(lambda device: go_arrival(step, device).wait_recv())
        for piece in range(2 * pieces):
            if step == 0:
                if piece < pieces:
                    for copy in own_copies(piece):
                        copy.wait()
                else:
                    for copy in half_copies(piece - pieces):
                        copy.wait_recv()
            add_piece(step, piece, piece == 0)
        results[step] = total[...].astype(jnp.bfloat16).reshape(experts, capacity, width)
        over_peers(lambda device: back_copy(step, device).start())
        returned[step, me] = results[step, me]
    for step in range(steps):
        combine(step)

    for piece in range(pieces):
        for copy in half_copies(piece):
            copy.wait_send()
    for step in range(steps):
        over_peers(lambda device: go_copy(step, device).wait_send())
        over_peers(lambda device: back_copy(step, device).wait_send())


def kernel_layer(states, language, placement, swap_flags, up_local, down_local, experts, capacity):
    steps, rows, width = states.shape
    pieces = up_local.shape[1] // PIECE
    blocks = pltpu.VMEM((steps, experts, capacity, width), jnp.bfloat16)
    sems = pltpu.SemaphoreType.DMA
    vmem = pl.BlockSpec(memory_space=pltpu.VMEM)
    anywhere = pl.BlockSpec(memory_space=pl.ANY)
    update = pl.pallas_call(
        layer_kernel,
        out_shape=jax.ShapeDtypeStruct((steps, rows, width), jnp.bfloat16),
        in_specs=[vmem, vmem, vmem, vmem, anywhere, anywhere],
        out_specs=vmem,
        scratch_shapes=[
            pltpu.VMEM((2 * pieces, width, PIECE), jnp.bfloat16),
            pltpu.VMEM((2 * pieces, PIECE, width), jnp.bfloat16),
            blocks, blocks, blocks, blocks,
            pltpu.VMEM((steps, experts * capacity, rows), jnp.bfloat16),
            pltpu.VMEM((experts * capacity, width), jnp.float32),
            sems((2, pieces)), sems((2, pieces)), sems((2, pieces)),
            sems((steps, experts)), sems((steps, experts)),
            sems((steps, experts)), sems((steps, experts)),
        ],
        compiler_params=pltpu.CompilerParams(
            collective_id=0, has_side_effects=True, vmem_limit_bytes=56 * 2**20),
        cost_estimate=pl.CostEstimate(
            flops=8 * steps * experts * capacity * width * up_local.shape[1],
            bytes_accessed=4 * up_local.size * 2, transcendentals=0),
    )(language.reshape(steps, 1, rows), placement, swap_flags[None, :], states, up_local, down_local)
    return (states.astype(jnp.float32) + update.astype(jnp.float32)).astype(jnp.bfloat16)


def plain_layer(states, language, placement, swap_flags, up_local, down_local, experts, capacity):
    slot_index = slots_of(language, placement, swap_flags, experts, capacity)
    width = states.shape[2]
    slot_labels = jnp.arange(experts * capacity, dtype=jnp.int32)
    outputs = []
    for step in range(states.shape[0]):
        select = (slot_index[step][:, None] == slot_labels[None, :]).astype(jnp.bfloat16)
        outgoing = jnp.einsum("rs,rd->sd", select, states[step], preferred_element_type=jnp.float32)
        arrived = lax.all_to_all(
            outgoing.astype(jnp.bfloat16).reshape(experts, capacity, width),
            "expert", split_axis=0, concat_axis=0, tiled=True)
        both = lax.all_gather(
            arrived.reshape(experts * capacity, width), "dp", axis=0, tiled=True)
        hidden = jnp.maximum(jnp.dot(both, up_local, preferred_element_type=jnp.float32), 0.0)
        terms = jnp.dot(hidden.astype(jnp.bfloat16), down_local, preferred_element_type=jnp.float32)
        served = lax.psum_scatter(terms, "dp", scatter_dimension=0, tiled=True).astype(jnp.bfloat16)
        returned = lax.all_to_all(
            served.reshape(experts, capacity, width), "expert", split_axis=0, concat_axis=0, tiled=True)
        update = jnp.dot(
            select, returned.reshape(experts * capacity, width), preferred_element_type=jnp.float32)
        outputs.append((states[step].astype(jnp.float32) + update).astype(jnp.bfloat16))
    return jnp.stack(outputs)


def shards(states, language, placement, swap_flags, up_weight, down_weight):
    experts = lax.axis_size("expert")
    capacity = max(2, 2 * states.shape[1] // experts)
    layer = kernel_layer if capacity % 16 == 0 else plain_layer
    return layer(states, language, placement, swap_flags, up_weight[0], down_weight[0], experts, capacity)


def solution(mesh):
    rows_by = P(None, ("dp", "expert"), None)
    return jax.shard_map(
        shards,
        mesh=mesh,
        in_specs=(rows_by, rows_by, P(), P(), P("expert", None, "dp"), P("expert", "dp", None)),
        out_specs=rows_by,
        check_vma=False,
    )
```

```python
import jax
import jax.numpy as jnp
from jax import lax
from jax.experimental import pallas as pl
from jax.experimental.pallas import tpu as pltpu
from jax.sharding import PartitionSpec as P

MESH = pl.DeviceIdType.MESH
PIECE = 512


def slots_of(language, placement, swap_flags, experts, capacity):
    labels = jnp.arange(experts, dtype=jnp.int32)
    resident = jnp.where(swap_flags == 1, (labels + experts // 2) % experts, labels)
    moved = jnp.sum(jnp.where(placement[:, :, None] == labels, resident, 0), axis=2)
    steps = jnp.arange(placement.shape[0], dtype=jnp.int32)[:, None]
    device_of = jnp.where(steps == 0, placement, moved)
    ids = language[:, :, 0]
    target = jnp.sum(jnp.where(ids[:, :, None] == labels, device_of[:, None, :], 0), axis=2)
    rows = jnp.arange(ids.shape[1], dtype=jnp.int32)
    earlier = (ids[:, :, None] == ids[:, None, :]) & (rows[None, :] < rows[:, None])
    return target * capacity + jnp.sum(earlier.astype(jnp.int32), axis=2)


def layer_kernel(
    language, placement, swap_flags, states, up, down, out,
    up_all, down_all, outgoing, arrived, results, returned, picks, total,
    own_sem, half_send, half_recv, go_send, go_recv, back_send, back_recv,
):
    steps, experts, capacity, width = outgoing.shape
    pieces = up_all.shape[0] // 2
    rows = states.shape[1]
    slots = experts * capacity
    core, me = lax.axis_index("dp"), lax.axis_index("expert")
    other = 1 - core

    def peer(k):
        return lax.rem(me + k, experts)

    def over_peers(body):
        def step_of(k, carry):
            body(peer(k))
            return carry
        lax.fori_loop(1, experts, step_of, 0)

    def own_copies(piece):
        columns = pl.ds(piece * PIECE, PIECE)
        return (
            pltpu.make_async_copy(up.at[:, columns], up_all.at[piece], own_sem.at[0, piece]),
            pltpu.make_async_copy(down.at[columns, :], down_all.at[piece], own_sem.at[1, piece]),
        )

    def half_copies(piece):
        columns = pl.ds(piece * PIECE, PIECE)
        ends = dict(device_id=(other, me), device_id_type=MESH)
        return (
            pltpu.make_async_remote_copy(
                up.at[:, columns], up_all.at[pieces + piece], half_send.at[0, piece], half_recv.at[0, piece], **ends),
            pltpu.make_async_remote_copy(
                down.at[columns, :], down_all.at[pieces + piece], half_send.at[1, piece], half_recv.at[1, piece], **ends),
        )

    def go_copy(step, device):
        return pltpu.make_async_remote_copy(
            outgoing.at[step, device], arrived.at[step, me], go_send.at[step, device], go_recv.at[step, me],
            device_id=(core, device), device_id_type=MESH)

    def go_arrival(step, device):
        return pltpu.make_async_remote_copy(
            outgoing.at[step, device], arrived.at[step, device], go_send.at[step, device], go_recv.at[step, device],
            device_id=(core, device), device_id_type=MESH)

    def back_copy(step, device):
        return pltpu.make_async_remote_copy(
            results.at[step, device], returned.at[step, me], back_send.at[step, device], back_recv.at[step, me],
            device_id=(core, device), device_id_type=MESH)

    def back_arrival(step, device):
        return pltpu.make_async_remote_copy(
            results.at[step, device], returned.at[step, device], back_send.at[step, device], back_recv.at[step, device],
            device_id=(core, device), device_id_type=MESH)

    barrier = pltpu.get_barrier_semaphore()
    over_peers(lambda device: pl.semaphore_signal(
        barrier, inc=1, device_id=(core, device), device_id_type=MESH))
    pl.semaphore_signal(barrier, inc=1, device_id=(other, me), device_id_type=MESH)

    def fill(step):
        langs = placement.shape[1]
        label = lax.broadcasted_iota(jnp.int32, (langs, langs), 0)
        along = lax.broadcasted_iota(jnp.int32, (langs, langs), 1)
        served_by = placement[pl.ds(step, 1), :].astype(jnp.float32)
        target = jnp.sum(jnp.where(label == along, served_by, 0.0), axis=1, keepdims=True)
        if step:
            flags = swap_flags[...].astype(jnp.float32)
            flag = jnp.sum(
                jnp.where(along.astype(jnp.float32) == target, flags, 0.0), axis=1, keepdims=True)
            half = experts // 2
            traded = jnp.where(target < half, target + half, target - half)
            target = jnp.where(flag > 0.5, traded, target)
        hot = lax.broadcasted_iota(jnp.int32, (langs, rows), 0) == language[step]
        before = (lax.broadcasted_iota(jnp.int32, (rows, rows), 0)
                  < lax.broadcasted_iota(jnp.int32, (rows, rows), 1))
        earlier = jnp.dot(
            hot.astype(jnp.bfloat16), before.astype(jnp.bfloat16), preferred_element_type=jnp.float32)
        slot = jnp.sum(jnp.where(hot, target * capacity + earlier, 0.0), axis=0, keepdims=True)
        place = lax.broadcasted_iota(jnp.int32, (slots, rows), 0)
        pick = (place == slot.astype(jnp.int32)).astype(jnp.bfloat16)
        picks[step] = pick
        rows_out = jnp.dot(pick, states[step], preferred_element_type=jnp.float32)
        outgoing[step] = rows_out.astype(jnp.bfloat16).reshape(experts, capacity, width)

    def send(step):
        over_peers(lambda device: go_copy(step, device).start())
        arrived[step, me] = outgoing[step, me]

    fill(0)
    pl.semaphore_wait(barrier, experts)
    send(0)
    for piece in range(pieces):
        for copy in own_copies(piece) + half_copies(piece):
            copy.start()
    for step in range(1, steps):
        fill(step)
        if step == 1:
            send(step)

    def add_piece(step, piece, first):
        x = arrived[step].reshape(slots, width)
        hidden = jnp.dot(x, up_all[piece], preferred_element_type=jnp.float32)
        hidden = jnp.maximum(hidden, 0.0).astype(jnp.bfloat16)
        term = jnp.dot(hidden, down_all[piece], preferred_element_type=jnp.float32)
        if first:
            total[...] = term
        else:
            total[...] += term

    def combine(step):
        over_peers(lambda device: back_arrival(step, device).wait_recv())
        update = lax.dot_general(
            picks[step], returned[step].reshape(slots, width), (((0,), (0,)), ((), ())),
            preferred_element_type=jnp.float32)
        out[step] = update.astype(jnp.bfloat16)

    for step in range(steps):
        over_peers(lambda device: go_arrival(step, device).wait_recv())
        if step + 2 < steps:
            send(step + 2)
        for piece in range(2 * pieces):
            if step == 0:
                if piece < pieces:
                    for copy in own_copies(piece):
                        copy.wait()
                else:
                    for copy in half_copies(piece - pieces):
                        copy.wait_recv()
            add_piece(step, piece, piece == 0)
        results[step] = total[...].astype(jnp.bfloat16).reshape(experts, capacity, width)
        over_peers(lambda device: back_copy(step, device).start())
        returned[step, me] = results[step, me]
    for step in range(steps):
        combine(step)

    for piece in range(pieces):
        for copy in half_copies(piece):
            copy.wait_send()
    for step in range(steps):
        over_peers(lambda device: go_copy(step, device).wait_send())
        over_peers(lambda device: back_copy(step, device).wait_send())


def kernel_layer(states, language, placement, swap_flags, up_local, down_local, experts, capacity):
    steps, rows, width = states.shape
    pieces = up_local.shape[1] // PIECE
    blocks = pltpu.VMEM((steps, experts, capacity, width), jnp.bfloat16)
    sems = pltpu.SemaphoreType.DMA
    vmem = pl.BlockSpec(memory_space=pltpu.VMEM)
    anywhere = pl.BlockSpec(memory_space=pl.ANY)
    update = pl.pallas_call(
        layer_kernel,
        out_shape=pltpu.VMEM((steps, rows, width), jnp.bfloat16),
        in_specs=[vmem, vmem, vmem, vmem, anywhere, anywhere],
        out_specs=vmem,
        scratch_shapes=[
            pltpu.VMEM((2 * pieces, width, PIECE), jnp.bfloat16),
            pltpu.VMEM((2 * pieces, PIECE, width), jnp.bfloat16),
            blocks, blocks, blocks, blocks,
            pltpu.VMEM((steps, experts * capacity, rows), jnp.bfloat16),
            pltpu.VMEM((experts * capacity, width), jnp.float32),
            sems((2, pieces)), sems((2, pieces)), sems((2, pieces)),
            sems((steps, experts)), sems((steps, experts)),
            sems((steps, experts)), sems((steps, experts)),
        ],
        compiler_params=pltpu.CompilerParams(
            collective_id=0, has_side_effects=True, vmem_limit_bytes=56 * 2**20),
        cost_estimate=pl.CostEstimate(
            flops=8 * steps * experts * capacity * width * up_local.shape[1],
            bytes_accessed=4 * up_local.size * 2, transcendentals=0),
    )(language.reshape(steps, 1, rows), placement, swap_flags[None, :], states, up_local, down_local)
    return (states.astype(jnp.float32) + update.astype(jnp.float32)).astype(jnp.bfloat16)


def plain_layer(states, language, placement, swap_flags, up_local, down_local, experts, capacity):
    slot_index = slots_of(language, placement, swap_flags, experts, capacity)
    width = states.shape[2]
    slot_labels = jnp.arange(experts * capacity, dtype=jnp.int32)
    outputs = []
    for step in range(states.shape[0]):
        select = (slot_index[step][:, None] == slot_labels[None, :]).astype(jnp.bfloat16)
        outgoing = jnp.einsum("rs,rd->sd", select, states[step], preferred_element_type=jnp.float32)
        arrived = lax.all_to_all(
            outgoing.astype(jnp.bfloat16).reshape(experts, capacity, width),
            "expert", split_axis=0, concat_axis=0, tiled=True)
        both = lax.all_gather(
            arrived.reshape(experts * capacity, width), "dp", axis=0, tiled=True)
        hidden = jnp.maximum(jnp.dot(both, up_local, preferred_element_type=jnp.float32), 0.0)
        terms = jnp.dot(hidden.astype(jnp.bfloat16), down_local, preferred_element_type=jnp.float32)
        served = lax.psum_scatter(terms, "dp", scatter_dimension=0, tiled=True).astype(jnp.bfloat16)
        returned = lax.all_to_all(
            served.reshape(experts, capacity, width), "expert", split_axis=0, concat_axis=0, tiled=True)
        update = jnp.dot(
            select, returned.reshape(experts * capacity, width), preferred_element_type=jnp.float32)
        outputs.append((states[step].astype(jnp.float32) + update).astype(jnp.bfloat16))
    return jnp.stack(outputs)


def shards(states, language, placement, swap_flags, up_weight, down_weight):
    experts = lax.axis_size("expert")
    capacity = max(2, 2 * states.shape[1] // experts)
    layer = kernel_layer if capacity % 16 == 0 else plain_layer
    return layer(states, language, placement, swap_flags, up_weight[0], down_weight[0], experts, capacity)


def solution(mesh):
    rows_by = P(None, ("dp", "expert"), None)
    return jax.shard_map(
        shards,
        mesh=mesh,
        in_specs=(rows_by, rows_by, P(), P(), P("expert", None, "dp"), P("expert", "dp", None)),
        out_specs=rows_by,
        check_vma=False,
    )
```

```python
import jax
import jax.numpy as jnp
from jax import lax
from jax.experimental import pallas as pl
from jax.experimental.pallas import tpu as pltpu
from jax.sharding import PartitionSpec as P

MESH = pl.DeviceIdType.MESH
PIECE = 512


def slots_of(language, placement, swap_flags, experts, capacity):
    labels = jnp.arange(experts, dtype=jnp.int32)
    resident = jnp.where(swap_flags == 1, (labels + experts // 2) % experts, labels)
    moved = jnp.sum(jnp.where(placement[:, :, None] == labels, resident, 0), axis=2)
    steps = jnp.arange(placement.shape[0], dtype=jnp.int32)[:, None]
    device_of = jnp.where(steps == 0, placement, moved)
    ids = language[:, :, 0]
    target = jnp.sum(jnp.where(ids[:, :, None] == labels, device_of[:, None, :], 0), axis=2)
    rows = jnp.arange(ids.shape[1], dtype=jnp.int32)
    earlier = (ids[:, :, None] == ids[:, None, :]) & (rows[None, :] < rows[:, None])
    return target * capacity + jnp.sum(earlier.astype(jnp.int32), axis=2)


def layer_kernel(
    language, placement, swap_flags, states_in, up, down, out,
    up_all, down_all, outgoing, arrived, results, returned, picks, total, states,
    state_sem, own_sem, half_send, half_recv, go_send, go_recv, back_send, back_recv,
):
    steps, experts, capacity, width = outgoing.shape
    pieces = up_all.shape[0] // 2
    rows = states.shape[1]
    slots = experts * capacity
    core, me = lax.axis_index("dp"), lax.axis_index("expert")
    other = 1 - core

    def peer(k):
        return lax.rem(me + k, experts)

    def send_over_peers(body):
        if experts & (experts - 1):
            return over_peers(body)
        bits = [1 << place for place in range(experts.bit_length() - 1)]
        flips = [bit - 2 * bit * lax.rem(lax.div(me, bit), 2) for bit in bits]
        for turn in range(experts - 1):
            offset = (turn + 1) // 2 + (0 if turn % 2 else experts // 2)
            body(me + sum(flip for bit, flip in zip(bits, flips) if offset & bit))

    def over_peers(body):
        def step_of(k, carry):
            body(peer(k))
            return carry
        lax.fori_loop(1, experts, step_of, 0)

    def own_copies(piece):
        columns = pl.ds(piece * PIECE, PIECE)
        return (
            pltpu.make_async_copy(up.at[:, columns], up_all.at[piece], own_sem.at[0, piece]),
            pltpu.make_async_copy(down.at[columns, :], down_all.at[piece], own_sem.at[1, piece]),
        )

    def half_copies(piece):
        columns = pl.ds(piece * PIECE, PIECE)
        ends = dict(device_id=(other, me), device_id_type=MESH)
        return (
            pltpu.make_async_remote_copy(
                up.at[:, columns], up_all.at[pieces + piece], half_send.at[0, piece], half_recv.at[0, piece], **ends),
            pltpu.make_async_remote_copy(
                down.at[columns, :], down_all.at[pieces + piece], half_send.at[1, piece], half_recv.at[1, piece], **ends),
        )

    def go_copy(step, device):
        return pltpu.make_async_remote_copy(
            outgoing.at[step, device], arrived.at[step, me], go_send.at[step, device], go_recv.at[step, me],
            device_id=(core, device), device_id_type=MESH)

    def go_arrival(step, device):
        return pltpu.make_async_remote_copy(
            outgoing.at[step, device], arrived.at[step, device], go_send.at[step, device], go_recv.at[step, device],
            device_id=(core, device), device_id_type=MESH)

    def back_copy(step, device):
        return pltpu.make_async_remote_copy(
            results.at[step, device], returned.at[step, me], back_send.at[step, device], back_recv.at[step, me],
            device_id=(core, device), device_id_type=MESH)

    def back_arrival(step, device):
        return pltpu.make_async_remote_copy(
            results.at[step, device], returned.at[step, device], back_send.at[step, device], back_recv.at[step, device],
            device_id=(core, device), device_id_type=MESH)

    def state_copy(step):
        return pltpu.make_async_copy(states_in.at[step], states.at[step], state_sem.at[step])

    for step in range(steps):
        state_copy(step).start()
    barrier = pltpu.get_barrier_semaphore()
    over_peers(lambda device: pl.semaphore_signal(
        barrier, inc=1, device_id=(core, device), device_id_type=MESH))
    pl.semaphore_signal(barrier, inc=1, device_id=(other, me), device_id_type=MESH)

    def fill(step):
        langs = placement.shape[1]
        label = lax.broadcasted_iota(jnp.int32, (langs, langs), 0)
        along = lax.broadcasted_iota(jnp.int32, (langs, langs), 1)
        served_by = placement[pl.ds(step, 1), :].astype(jnp.float32)
        target = jnp.sum(jnp.where(label == along, served_by, 0.0), axis=1, keepdims=True)
        if step:
            flags = swap_flags[...].astype(jnp.float32)
            flag = jnp.sum(
                jnp.where(along.astype(jnp.float32) == target, flags, 0.0), axis=1, keepdims=True)
            half = experts // 2
            traded = jnp.where(target < half, target + half, target - half)
            target = jnp.where(flag > 0.5, traded, target)
        hot = lax.broadcasted_iota(jnp.int32, (langs, rows), 0) == language[step]
        before = (lax.broadcasted_iota(jnp.int32, (rows, rows), 0)
                  < lax.broadcasted_iota(jnp.int32, (rows, rows), 1))
        earlier = jnp.dot(
            hot.astype(jnp.bfloat16), before.astype(jnp.bfloat16), preferred_element_type=jnp.float32)
        slot = jnp.sum(jnp.where(hot, target * capacity + earlier, 0.0), axis=0, keepdims=True)
        place = lax.broadcasted_iota(jnp.int32, (slots, rows), 0)
        pick = (place == slot.astype(jnp.int32)).astype(jnp.bfloat16)
        picks[step] = pick
        state_copy(step).wait()
        rows_out = jnp.dot(pick, states[step], preferred_element_type=jnp.float32)
        outgoing[step] = rows_out.astype(jnp.bfloat16).reshape(experts, capacity, width)

    def send(step):
        send_over_peers(lambda device: go_copy(step, device).start())
        arrived[step, me] = outgoing[step, me]

    fill(0)
    pl.semaphore_wait(barrier, experts)
    send(0)
    for piece in range(pieces):
        for copy in own_copies(piece) + half_copies(piece):
            copy.start()
    for step in range(1, steps):
        fill(step)
        if step == 1:
            send(step)

    def add_piece(step, piece, first):
        x = arrived[step].reshape(slots, width)
        hidden = jnp.dot(x, up_all[piece], preferred_element_type=jnp.float32)
        hidden = jnp.maximum(hidden, 0.0).astype(jnp.bfloat16)
        term = jnp.dot(hidden, down_all[piece], preferred_element_type=jnp.float32)
        if first:
            total[...] = term
        else:
            total[...] += term

    def combine(step):
        over_peers(lambda device: back_arrival(step, device).wait_recv())
        update = lax.dot_general(
            picks[step], returned[step].reshape(slots, width), (((0,), (0,)), ((), ())),
            preferred_element_type=jnp.float32)
        out[step] = update.astype(jnp.bfloat16)

    for step in range(steps):
        over_peers(lambda device: go_arrival(step, device).wait_recv())
        if step + 2 < steps:
            send(step + 2)
        for piece in range(2 * pieces):
            if step == 0:
                if piece < pieces:
                    for copy in own_copies(piece):
                        copy.wait()
                else:
                    for copy in half_copies(piece - pieces):
                        copy.wait_recv()
            add_piece(step, piece, piece == 0)
        results[step] = total[...].astype(jnp.bfloat16).reshape(experts, capacity, width)
        send_over_peers(lambda device: back_copy(step, device).start())
        returned[step, me] = results[step, me]
    for step in range(steps):
        combine(step)

    for piece in range(pieces):
        for copy in half_copies(piece):
            copy.wait_send()
    for step in range(steps):
        over_peers(lambda device: go_copy(step, device).wait_send())
        over_peers(lambda device: back_copy(step, device).wait_send())


def kernel_layer(states, language, placement, swap_flags, up_local, down_local, experts, capacity):
    steps, rows, width = states.shape
    pieces = up_local.shape[1] // PIECE
    blocks = pltpu.VMEM((steps, experts, capacity, width), jnp.bfloat16)
    sems = pltpu.SemaphoreType.DMA
    vmem = pl.BlockSpec(memory_space=pltpu.VMEM)
    anywhere = pl.BlockSpec(memory_space=pl.ANY)
    update = pl.pallas_call(
        layer_kernel,
        out_shape=pltpu.VMEM((steps, rows, width), jnp.bfloat16),
        in_specs=[vmem, vmem, vmem, anywhere, anywhere, anywhere],
        out_specs=vmem,
        scratch_shapes=[
            pltpu.VMEM((2 * pieces, width, PIECE), jnp.bfloat16),
            pltpu.VMEM((2 * pieces, PIECE, width), jnp.bfloat16),
            blocks, blocks, blocks, blocks,
            pltpu.VMEM((steps, experts * capacity, rows), jnp.bfloat16),
            pltpu.VMEM((experts * capacity, width), jnp.float32),
            pltpu.VMEM(states.shape, states.dtype),
            sems((steps,)), sems((2, pieces)), sems((2, pieces)), sems((2, pieces)),
            sems((steps, experts)), sems((steps, experts)),
            sems((steps, experts)), sems((steps, experts)),
        ],
        compiler_params=pltpu.CompilerParams(
            collective_id=0, has_side_effects=True, vmem_limit_bytes=56 * 2**20),
        cost_estimate=pl.CostEstimate(
            flops=8 * steps * experts * capacity * width * up_local.shape[1],
            bytes_accessed=4 * up_local.size * 2, transcendentals=0),
    )(language.reshape(steps, 1, rows), placement, swap_flags[None, :], states, up_local, down_local)
    return (states.astype(jnp.float32) + update.astype(jnp.float32)).astype(jnp.bfloat16)


def plain_layer(states, language, placement, swap_flags, up_local, down_local, experts, capacity):
    slot_index = slots_of(language, placement, swap_flags, experts, capacity)
    width = states.shape[2]
    slot_labels = jnp.arange(experts * capacity, dtype=jnp.int32)
    outputs = []
    for step in range(states.shape[0]):
        select = (slot_index[step][:, None] == slot_labels[None, :]).astype(jnp.bfloat16)
        outgoing = jnp.einsum("rs,rd->sd", select, states[step], preferred_element_type=jnp.float32)
        arrived = lax.all_to_all(
            outgoing.astype(jnp.bfloat16).reshape(experts, capacity, width),
            "expert", split_axis=0, concat_axis=0, tiled=True)
        both = lax.all_gather(
            arrived.reshape(experts * capacity, width), "dp", axis=0, tiled=True)
        hidden = jnp.maximum(jnp.dot(both, up_local, preferred_element_type=jnp.float32), 0.0)
        terms = jnp.dot(hidden.astype(jnp.bfloat16), down_local, preferred_element_type=jnp.float32)
        served = lax.psum_scatter(terms, "dp", scatter_dimension=0, tiled=True).astype(jnp.bfloat16)
        returned = lax.all_to_all(
            served.reshape(experts, capacity, width), "expert", split_axis=0, concat_axis=0, tiled=True)
        update = jnp.dot(
            select, returned.reshape(experts * capacity, width), preferred_element_type=jnp.float32)
        outputs.append((states[step].astype(jnp.float32) + update).astype(jnp.bfloat16))
    return jnp.stack(outputs)


def shards(states, language, placement, swap_flags, up_weight, down_weight):
    experts = lax.axis_size("expert")
    capacity = max(2, 2 * states.shape[1] // experts)
    layer = kernel_layer if capacity % 16 == 0 else plain_layer
    return layer(states, language, placement, swap_flags, up_weight[0], down_weight[0], experts, capacity)


def solution(mesh):
    rows_by = P(None, ("dp", "expert"), None)
    return jax.shard_map(
        shards,
        mesh=mesh,
        in_specs=(rows_by, rows_by, P(), P(), P("expert", None, "dp"), P("expert", "dp", None)),
        out_specs=rows_by,
        check_vma=False,
    )
```

```python
import jax
import jax.numpy as jnp
from jax import lax
from jax.experimental import pallas as pl
from jax.experimental.pallas import tpu as pltpu
from jax.sharding import PartitionSpec as P

MESH = pl.DeviceIdType.MESH
PIECE = 512


def slots_of(language, placement, swap_flags, experts, capacity):
    labels = jnp.arange(experts, dtype=jnp.int32)
    resident = jnp.where(swap_flags == 1, (labels + experts // 2) % experts, labels)
    moved = jnp.sum(jnp.where(placement[:, :, None] == labels, resident, 0), axis=2)
    steps = jnp.arange(placement.shape[0], dtype=jnp.int32)[:, None]
    device_of = jnp.where(steps == 0, placement, moved)
    ids = language[:, :, 0]
    target = jnp.sum(jnp.where(ids[:, :, None] == labels, device_of[:, None, :], 0), axis=2)
    rows = jnp.arange(ids.shape[1], dtype=jnp.int32)
    earlier = (ids[:, :, None] == ids[:, None, :]) & (rows[None, :] < rows[:, None])
    return target * capacity + jnp.sum(earlier.astype(jnp.int32), axis=2)


def layer_kernel(
    language, placement, swap_flags, states, up, down, out,
    up_all, down_all, outgoing, arrived, results, returned, picks, total,
    own_sem, half_send, half_recv, go_send, go_recv, back_send, back_recv,
):
    steps, experts, capacity, width = outgoing.shape
    pieces = up_all.shape[0] // 2
    rows = states.shape[1]
    slots = experts * capacity
    core, me = lax.axis_index("dp"), lax.axis_index("expert")
    other = 1 - core

    def peer(k):
        return lax.rem(me + k + core * (experts - 2 * k), experts)

    def over_peers(body):
        def step_of(k, carry):
            body(peer(k))
            return carry
        lax.fori_loop(1, experts, step_of, 0)

    def own_copies(piece):
        columns = pl.ds(piece * PIECE, PIECE)
        return (
            pltpu.make_async_copy(up.at[:, columns], up_all.at[piece], own_sem.at[0, piece]),
            pltpu.make_async_copy(down.at[columns, :], down_all.at[piece], own_sem.at[1, piece]),
        )

    def half_copies(piece):
        columns = pl.ds(piece * PIECE, PIECE)
        ends = dict(device_id=(other, me), device_id_type=MESH)
        return (
            pltpu.make_async_remote_copy(
                up.at[:, columns], up_all.at[pieces + piece], half_send.at[0, piece], half_recv.at[0, piece], **ends),
            pltpu.make_async_remote_copy(
                down.at[columns, :], down_all.at[pieces + piece], half_send.at[1, piece], half_recv.at[1, piece], **ends),
        )

    def go_copy(step, device):
        return pltpu.make_async_remote_copy(
            outgoing.at[step, device], arrived.at[step, me], go_send.at[step, device], go_recv.at[step, me],
            device_id=(core, device), device_id_type=MESH)

    def go_arrival(step, device):
        return pltpu.make_async_remote_copy(
            outgoing.at[step, device], arrived.at[step, device], go_send.at[step, device], go_recv.at[step, device],
            device_id=(core, device), device_id_type=MESH)

    def back_copy(step, device):
        return pltpu.make_async_remote_copy(
            results.at[step, device], returned.at[step, me], back_send.at[step, device], back_recv.at[step, me],
            device_id=(core, device), device_id_type=MESH)

    def back_arrival(step, device):
        return pltpu.make_async_remote_copy(
            results.at[step, device], returned.at[step, device], back_send.at[step, device], back_recv.at[step, device],
            device_id=(core, device), device_id_type=MESH)

    barrier = pltpu.get_barrier_semaphore()
    over_peers(lambda device: pl.semaphore_signal(
        barrier, inc=1, device_id=(core, device), device_id_type=MESH))
    pl.semaphore_signal(barrier, inc=1, device_id=(other, me), device_id_type=MESH)

    def fill(step):
        langs = placement.shape[1]
        label = lax.broadcasted_iota(jnp.int32, (langs, langs), 0)
        along = lax.broadcasted_iota(jnp.int32, (langs, langs), 1)
        served_by = placement[pl.ds(step, 1), :].astype(jnp.float32)
        target = jnp.sum(jnp.where(label == along, served_by, 0.0), axis=1, keepdims=True)
        if step:
            flags = swap_flags[...].astype(jnp.float32)
            flag = jnp.sum(
                jnp.where(along.astype(jnp.float32) == target, flags, 0.0), axis=1, keepdims=True)
            half = experts // 2
            traded = jnp.where(target < half, target + half, target - half)
            target = jnp.where(flag > 0.5, traded, target)
        hot = lax.broadcasted_iota(jnp.int32, (langs, rows), 0) == language[step]
        before = (lax.broadcasted_iota(jnp.int32, (rows, rows), 0)
                  < lax.broadcasted_iota(jnp.int32, (rows, rows), 1))
        earlier = jnp.dot(
            hot.astype(jnp.bfloat16), before.astype(jnp.bfloat16), preferred_element_type=jnp.float32)
        slot = jnp.sum(jnp.where(hot, target * capacity + earlier, 0.0), axis=0, keepdims=True)
        place = lax.broadcasted_iota(jnp.int32, (slots, rows), 0)
        pick = (place == slot.astype(jnp.int32)).astype(jnp.bfloat16)
        picks[step] = pick
        rows_out = jnp.dot(pick, states[step], preferred_element_type=jnp.float32)
        outgoing[step] = rows_out.astype(jnp.bfloat16).reshape(experts, capacity, width)

    def send(step):
        over_peers(lambda device: go_copy(step, device).start())
        arrived[step, me] = outgoing[step, me]

    fill(0)
    pl.semaphore_wait(barrier, experts)
    send(0)
    for piece in range(pieces):
        for copy in own_copies(piece) + half_copies(piece):
            copy.start()
    for step in range(1, steps):
        fill(step)
        if step == 1:
            send(step)

    def add_piece(step, piece, first):
        x = arrived[step].reshape(slots, width)
        hidden = jnp.dot(x, up_all[piece], preferred_element_type=jnp.float32)
        hidden = jnp.maximum(hidden, 0.0).astype(jnp.bfloat16)
        term = jnp.dot(hidden, down_all[piece], preferred_element_type=jnp.float32)
        if first:
            total[...] = term
        else:
            total[...] += term

    def combine(step):
        over_peers(lambda device: back_arrival(step, device).wait_recv())
        update = lax.dot_general(
            picks[step], returned[step].reshape(slots, width), (((0,), (0,)), ((), ())),
            preferred_element_type=jnp.float32)
        out[step] = update.astype(jnp.bfloat16)

    for step in range(steps):
        over_peers(lambda device: go_arrival(step, device).wait_recv())
        if step + 2 < steps:
            send(step + 2)
        for piece in range(2 * pieces):
            if step == 0:
                if piece < pieces:
                    for copy in own_copies(piece):
                        copy.wait()
                else:
                    for copy in half_copies(piece - pieces):
                        copy.wait_recv()
            add_piece(step, piece, piece == 0)
        results[step] = total[...].astype(jnp.bfloat16).reshape(experts, capacity, width)
        over_peers(lambda device: back_copy(step, device).start())
        returned[step, me] = results[step, me]
    for step in range(steps):
        combine(step)

    for piece in range(pieces):
        for copy in half_copies(piece):
            copy.wait_send()
    for step in range(steps):
        over_peers(lambda device: go_copy(step, device).wait_send())
        over_peers(lambda device: back_copy(step, device).wait_send())


def kernel_layer(states, language, placement, swap_flags, up_local, down_local, experts, capacity):
    steps, rows, width = states.shape
    pieces = up_local.shape[1] // PIECE
    blocks = pltpu.VMEM((steps, experts, capacity, width), jnp.bfloat16)
    sems = pltpu.SemaphoreType.DMA
    vmem = pl.BlockSpec(memory_space=pltpu.VMEM)
    anywhere = pl.BlockSpec(memory_space=pl.ANY)
    update = pl.pallas_call(
        layer_kernel,
        out_shape=pltpu.VMEM((steps, rows, width), jnp.bfloat16),
        in_specs=[vmem, vmem, vmem, vmem, anywhere, anywhere],
        out_specs=vmem,
        scratch_shapes=[
            pltpu.VMEM((2 * pieces, width, PIECE), jnp.bfloat16),
            pltpu.VMEM((2 * pieces, PIECE, width), jnp.bfloat16),
            blocks, blocks, blocks, blocks,
            pltpu.VMEM((steps, experts * capacity, rows), jnp.bfloat16),
            pltpu.VMEM((experts * capacity, width), jnp.float32),
            sems((2, pieces)), sems((2, pieces)), sems((2, pieces)),
            sems((steps, experts)), sems((steps, experts)),
            sems((steps, experts)), sems((steps, experts)),
        ],
        compiler_params=pltpu.CompilerParams(
            collective_id=0, has_side_effects=True, vmem_limit_bytes=56 * 2**20),
        cost_estimate=pl.CostEstimate(
            flops=8 * steps * experts * capacity * width * up_local.shape[1],
            bytes_accessed=4 * up_local.size * 2, transcendentals=0),
    )(language.reshape(steps, 1, rows), placement, swap_flags[None, :], states, up_local, down_local)
    return (states.astype(jnp.float32) + update.astype(jnp.float32)).astype(jnp.bfloat16)


def plain_layer(states, language, placement, swap_flags, up_local, down_local, experts, capacity):
    slot_index = slots_of(language, placement, swap_flags, experts, capacity)
    width = states.shape[2]
    slot_labels = jnp.arange(experts * capacity, dtype=jnp.int32)
    outputs = []
    for step in range(states.shape[0]):
        select = (slot_index[step][:, None] == slot_labels[None, :]).astype(jnp.bfloat16)
        outgoing = jnp.einsum("rs,rd->sd", select, states[step], preferred_element_type=jnp.float32)
        arrived = lax.all_to_all(
            outgoing.astype(jnp.bfloat16).reshape(experts, capacity, width),
            "expert", split_axis=0, concat_axis=0, tiled=True)
        both = lax.all_gather(
            arrived.reshape(experts * capacity, width), "dp", axis=0, tiled=True)
        hidden = jnp.maximum(jnp.dot(both, up_local, preferred_element_type=jnp.float32), 0.0)
        terms = jnp.dot(hidden.astype(jnp.bfloat16), down_local, preferred_element_type=jnp.float32)
        served = lax.psum_scatter(terms, "dp", scatter_dimension=0, tiled=True).astype(jnp.bfloat16)
        returned = lax.all_to_all(
            served.reshape(experts, capacity, width), "expert", split_axis=0, concat_axis=0, tiled=True)
        update = jnp.dot(
            select, returned.reshape(experts * capacity, width), preferred_element_type=jnp.float32)
        outputs.append((states[step].astype(jnp.float32) + update).astype(jnp.bfloat16))
    return jnp.stack(outputs)


def shards(states, language, placement, swap_flags, up_weight, down_weight):
    experts = lax.axis_size("expert")
    capacity = max(2, 2 * states.shape[1] // experts)
    layer = kernel_layer if capacity % 16 == 0 else plain_layer
    return layer(states, language, placement, swap_flags, up_weight[0], down_weight[0], experts, capacity)


def solution(mesh):
    rows_by = P(None, ("dp", "expert"), None)
    return jax.shard_map(
        shards,
        mesh=mesh,
        in_specs=(rows_by, rows_by, P(), P(), P("expert", None, "dp"), P("expert", "dp", None)),
        out_specs=rows_by,
        check_vma=False,
    )
```
